32 devices in a mesh: ctx: 8 (over y, x, core), fsdp: 4 (over z).
Axes of the slice: x: 2, y: 2, z: 4, core: 2. Of those that a mesh axis runs over, the one named last changes fastest.
Arguments:
- queries: bfloat16 [6144, 3072], P('ctx', 'fsdp'), may hold values from -120 to 120
- key_input: bfloat16 [6144, 3072], P('ctx', 'fsdp'), may hold values from -120 to 120
- value_input: bfloat16 [6144, 3072], P('ctx', 'fsdp'), may hold values from -6 to 6
- out_grad: bfloat16 [6144, 3072], P('ctx', 'fsdp'), may hold values from -21 to 21
- norm_gains: float32 [3, 128], replicated, may hold values from 0.1 to 1.9
- block_lists: int32 [48, 5], P('ctx'), may hold values from -1 to 47, as said below
Outputs:
- attended: bfloat16 [6144, 3072], P('ctx', 'fsdp')
- query_grad: bfloat16 [6144, 3072], P('ctx', 'fsdp')
- key_grad: bfloat16 [6144, 3072], P('ctx', 'fsdp')
- value_grad: bfloat16 [6144, 3072], P('ctx', 'fsdp')
- gain_grad: float32 [3, 128], replicated
The draws below stay inside these ranges and needn't reach their ends.
Inputs may be any that keep to these rules, and one draw needn't show every extreme that they name: `block_lists`: row b holds, in this order, b, b - 1, b - 2, s and s - 3, where s = b - (b mod 3) - 1; any entry but the first may be -1 instead; an entry is -1 wherever that number would be negative, and the fourth entry is -1 wherever b mod 3 is 0 or 1.
All inputs are finite; a program needn't handle non-finite values.
Results may differ from the reference program's by a relative error of at most 0.014.
Values may be sent and summed in bfloat16 or wider, within the bound.
A program may use at most 128 MiB of HBM per device.

```python
import math
import jax
import jax.numpy as jnp
import numpy as np
from jax import lax

HEADS = 24
HD = 128
BLOCK = 128
BLOCKS_DEV = 6
GROUP = 3
ROWS_DEV = 768
BLOCKS = 48
SEQ_LEN = 6144
WIDTH = 3072
N_CTX = 8


def scaled_field(key, base_field):
    row_key, col_key = jax.random.split(key, 2)
    row_scale = jnp.exp(jax.random.uniform(row_key, (SEQ_LEN, HEADS, 1), jnp.float32) * math.log(10.0))
    col_scale = jnp.exp(jax.random.uniform(col_key, (1, HEADS, HD), jnp.float32) * math.log(10.0))
    full_field = 0.3 * base_field * row_scale * col_scale
    return full_field.reshape(SEQ_LEN, HEADS * HD).astype(jnp.bfloat16)


def rough_projection(key, base_key):
    field_shape = (SEQ_LEN, HEADS, HD)
    base_field = jax.random.truncated_normal(base_key, -4.0, 4.0, field_shape, jnp.float32)
    return scaled_field(key, base_field)


def draw_queries(key, part):
    key = jax.random.fold_in(key, 11)
    base_key, rest_key = jax.random.split(key)
    return rough_projection(rest_key, base_key)


def draw_key_input(key, part):
    key = jax.random.fold_in(key, 13)
    base_key, rest_key = jax.random.split(key)
    return rough_projection(rest_key, base_key)


def ramped(base_field, power, amplitude):
    positions = (jnp.arange(SEQ_LEN, dtype=jnp.float32) / SEQ_LEN)[:, None]
    head_place = ((jnp.arange(HEADS * HD) // HD).astype(jnp.float32) / HEADS)[None, :]
    ramp = ((1.0 + 2.0 * positions) * (1.0 + 2.0 * head_place)) ** power
    return (amplitude * base_field * ramp).astype(jnp.bfloat16)


def draw_out_grad(key, part):
    key = jax.random.fold_in(key, 17)
    field_shape = (SEQ_LEN, HEADS * HD)
    base_field = jax.random.truncated_normal(key, -4.0, 4.0, field_shape, jnp.float32)
    return ramped(base_field, 1.0, 0.3)


def draw_block_lists(key, part):
    key = jax.random.fold_in(key, 19)
    numbers = jnp.arange(BLOCKS, dtype=jnp.int32)[:, None]
    within = numbers % GROUP
    summary = numbers - within - 1
    candidate = jnp.concatenate([numbers, numbers - 1, numbers - 2, summary, summary - GROUP], axis=1)
    columns = jnp.arange(5)[None, :]
    kept = jnp.logical_or(jax.random.randint(key, (BLOCKS, 5), 0, 4) != 0, columns == 0)
    repeated = jnp.logical_and(columns == 3, within < 2)
    usable = jnp.logical_and(jnp.logical_and(kept, candidate >= 0), jnp.logical_not(repeated))
    return jnp.where(usable, candidate, -1).astype(jnp.int32)


def level_of(key, dims, shards, smallest, high):
    gain, own = 1.0, jax.random.fold_in(key, 6)
    for axis_at, blocks in shards:
        steps = jnp.exp(jax.random.uniform(jax.random.fold_in(own, axis_at), (blocks,), jnp.float32, smallest / len(shards), high / len(shards)))
        gain = gain * jnp.repeat(steps, dims[axis_at] // blocks).reshape([-1 if axis == axis_at else 1 for axis in range(len(dims))])
    return gain


def noise(key, shape, deviation, most, shards=(), held_as=jnp.bfloat16):
    loudness = level_of(key, shape, shards, -0.22, 0.18) if shards else 1.0
    result = jax.random.normal(key, shape, jnp.float32) * deviation * loudness
    return jnp.minimum(jnp.maximum(result, -most), most).astype(held_as)


def setup_inputs(seed: int = 0) -> dict:
    keys = jax.random.split(jax.random.key(seed), 7)
    return {
        "queries": draw_queries(jax.random.fold_in(keys[6], 71), 0),
        "key_input": draw_key_input(jax.random.fold_in(keys[6], 71), 0),
        "value_input": noise(keys[2], (SEQ_LEN, WIDTH), 1.0, 6.0, ((0, 8), (1, 4))),
        "out_grad": draw_out_grad(jax.random.fold_in(keys[6], 71), 0),
        "norm_gains": jnp.clip(1.0 + 0.18 * jax.random.normal(keys[4], (3, HD), jnp.float32), 0.1, 1.9),
        "block_lists": draw_block_lists(jax.random.fold_in(keys[6], 71), 0),
    }


EPS = 1e-06

def unit_scale(raw_rows):
    return lax.rsqrt(lax.optimization_barrier(jnp.mean(raw_rows * raw_rows, axis=-1, keepdims=True)) + EPS)

def rounded_low(values_in):
    return lax.optimization_barrier(values_in.astype(jnp.bfloat16)).astype(jnp.float32)

def norm_backward(raw_rows, row_scale, gain_row, grad_norm):
    unit_rows = raw_rows * row_scale
    inner_grad = grad_norm * gain_row
    raw_grad = row_scale * (inner_grad - unit_rows * lax.optimization_barrier(jnp.mean(inner_grad * unit_rows, axis=-1, keepdims=True)))
    return (raw_grad, lax.optimization_barrier(jnp.sum(grad_norm * unit_rows, axis=(0, 1))))

def reference(queries, key_input, value_input, out_grad, norm_gains, block_lists):
    query_gain = norm_gains[0]
    key_gain = norm_gains[1]
    out_gain = norm_gains[2]
    key_all = key_input.astype(jnp.float32).reshape(SEQ_LEN, HEADS, HD)
    key_norm = (key_all * unit_scale(key_all) * key_gain).astype(jnp.bfloat16).reshape(BLOCKS, BLOCK, HEADS, HD)
    value_blocks = value_input.reshape(BLOCKS, BLOCK, HEADS, HD)
    tail_list = np.array([GROUP - 1, BLOCKS_DEV - 2, BLOCKS_DEV - 1], dtype=np.int32)
    inv_root = 1.0 / math.sqrt(HD)
    causal = jnp.arange(BLOCK)[:, None] >= jnp.arange(BLOCK)[None, :]
    diagonal_slot = (jnp.arange(5) == 0)[None, :, None]
    allowed = jnp.logical_or(jnp.logical_not(diagonal_slot), causal[:, None, :])

    def shard_step(carry, shard_parts):
        gain_carry, far_next = carry
        shard_index, query_shard, key_shard, grad_shard, lists = shard_parts
        start = (shard_index * BLOCKS_DEV).astype(jnp.int32)
        query_raw = query_shard.astype(jnp.float32).reshape(ROWS_DEV, HEADS, HD)
        key_raw = key_shard.astype(jnp.float32).reshape(ROWS_DEV, HEADS, HD)
        query_scale = unit_scale(query_raw)
        key_scale = unit_scale(key_raw)
        query_norm = rounded_low(query_raw * query_scale * query_gain).reshape(BLOCKS_DEV, BLOCK, HEADS, HD)
        key_index = jnp.maximum(lists, 0)
        present = lists >= 0
        gathered_keys = key_norm[key_index].astype(jnp.float32)
        gathered_values = value_blocks[key_index].astype(jnp.float32)
        scores = jnp.einsum('bthc,bjuhc->bhtju', query_norm, gathered_keys) * inv_root
        visible = jnp.logical_and(allowed[None, None], present[:, None, None, :, None])
        weights_raw = jnp.where(visible, jnp.exp(scores), 0.0)
        denominator = lax.optimization_barrier(jnp.sum(weights_raw, axis=(3, 4), keepdims=True))
        attention = weights_raw / denominator
        attention_low = rounded_low(attention)
        heads_out = jnp.einsum('bhtju,bjuhc->bthc', attention_low, gathered_values)
        attended = (heads_out * out_gain).astype(jnp.bfloat16).reshape(ROWS_DEV, WIDTH)
        grad_out = grad_shard.astype(jnp.float32).reshape(BLOCKS_DEV, BLOCK, HEADS, HD)
        out_term = lax.optimization_barrier(jnp.sum(grad_out * heads_out, axis=(0, 1, 2)))
        grad_heads = rounded_low(grad_out * out_gain)
        row_delta = lax.optimization_barrier(jnp.sum(grad_heads * heads_out, axis=-1))
        grad_attention = jnp.einsum('bthc,bjuhc->bhtju', grad_heads, gathered_values)
        delta_cols = jnp.transpose(row_delta, (0, 2, 1))[..., None, None]
        grad_scores = rounded_low(attention * (grad_attention - delta_cols) * inv_root)
        query_norm_grad = jnp.einsum('bhtju,bjuhc->bthc', grad_scores, gathered_keys)
        key_terms = jnp.einsum('bhtju,bthc->bjuhc', grad_scores, query_norm)
        value_terms = jnp.einsum('bhtju,bthc->bjuhc', attention_low, grad_heads)
        stacked = jnp.stack([key_terms, value_terms])
        local = (lists - start).astype(jnp.int32)
        own_index = jnp.where(local >= 0, local, BLOCKS_DEV).astype(jnp.int32)
        earlier = local + BLOCKS_DEV
        tail_slot = jnp.where(earlier == GROUP - 1, 0, jnp.where(earlier == BLOCKS_DEV - 2, 1, jnp.where(earlier == BLOCKS_DEV - 1, 2, 3)))
        tail_slot = jnp.where(local >= 0, 3, tail_slot).astype(jnp.int32)
        own_zero = jnp.zeros((2, BLOCKS_DEV + 1, BLOCK, HEADS, HD), jnp.float32)
        own_sum = own_zero.at[:, own_index].add(stacked)[:, :BLOCKS_DEV]
        far_zero = jnp.zeros((2, 4, BLOCK, HEADS, HD), jnp.float32)
        far_here = rounded_low(far_zero.at[:, tail_slot].add(stacked)[:, :3])
        key_side = own_sum.at[:, tail_list].add(far_next)
        key_norm_grad = key_side[0].reshape(ROWS_DEV, HEADS, HD)
        value_grad = key_side[1].astype(jnp.bfloat16).reshape(ROWS_DEV, WIDTH)
        query_grad, query_term = norm_backward(query_raw, query_scale, query_gain, query_norm_grad.reshape(ROWS_DEV, HEADS, HD))
        key_grad, key_term = norm_backward(key_raw, key_scale, key_gain, key_norm_grad)
        gain_terms = jnp.stack([query_term, key_term, out_term])
        outputs = (attended, query_grad.astype(jnp.bfloat16).reshape(ROWS_DEV, WIDTH), key_grad.astype(jnp.bfloat16).reshape(ROWS_DEV, WIDTH), value_grad)
        return ((gain_carry + gain_terms, far_here), outputs)
    shard_numbers = jnp.arange(N_CTX, dtype=jnp.int32)
    inputs = (shard_numbers, queries.reshape(N_CTX, ROWS_DEV, WIDTH), key_input.reshape(N_CTX, ROWS_DEV, WIDTH), out_grad.reshape(N_CTX, ROWS_DEV, WIDTH), block_lists.reshape(N_CTX, BLOCKS_DEV, 5))
    start_carry = (jnp.zeros((3, HD), jnp.float32), jnp.zeros((2, 3, BLOCK, HEADS, HD), jnp.float32))
    final_carry, outputs = lax.scan(shard_step, start_carry, inputs, reverse=True)
    gain_grad = final_carry[0] * (1.0 / math.sqrt(SEQ_LEN * HEADS))
    return (outputs[0].reshape(SEQ_LEN, WIDTH), outputs[1].reshape(SEQ_LEN, WIDTH), outputs[2].reshape(SEQ_LEN, WIDTH), outputs[3].reshape(SEQ_LEN, WIDTH), gain_grad)
```

```python
import functools
import math

import jax
import jax.numpy as jnp
from jax import lax
from jax.experimental import pallas as pl
from jax.experimental.pallas import tpu as pltpu
from jax.sharding import PartitionSpec as P

EPS = 1e-06
B = 128
D = 128
F32 = jnp.float32
BF16 = jnp.bfloat16
MESH = pl.DeviceIdType.MESH

KEYS = (-2, -4, -1, 0, 1, 2, 3, 4, 5)
SEEN = {-2: (0, 0), -4: (0, 2), -1: (0, 5), 0: (0, 2), 1: (1, 3), 2: (2, 5), 3: (3, 5), 4: (4, 5), 5: (5, 5)}
BASE = {}
_total = 0
for _key in KEYS:
    BASE[_key] = _total
    _total += SEEN[_key][1] - SEEN[_key][0] + 1
PAIRS = _total
WINDOW = []
for _b in range(6):
    _g = _b - _b % 3
    _low = {0: -1, 3: 2}[_g]
    _far = {0: -4, 3: -1}[_g]
    if _b % 3 == 0:
        WINDOW.append(((_b - 2, 2), (_far, 4), (_low, 1), (_b, 0)))
    elif _b % 3 == 1:
        WINDOW.append(((_far, 4), (_low, 2), (_b - 1, 1), (_b, 0)))
    else:
        WINDOW.append(((_far, 4), (_low, 3), (_b - 2, 2), (_b - 1, 1), (_b, 0)))
HALO_AT = {-4: 0, -2: 1, -1: 2}
TAIL = (2, 4, 5)
PIECES = ((2 * B, 0, B), (4 * B, B, 2 * B))


def rowmean(x):
    return jnp.sum(x, axis=-1, keepdims=True) * (1.0 / D)


def fold(x):
    return jnp.sum(x.reshape(x.shape[0] // 8, 8, D), axis=0)


def dot_nt(a, b):
    return lax.dot_general(a, b, (((1,), (1,)), ((), ())), preferred_element_type=F32)


def dot_nn(a, b):
    return lax.dot_general(a, b, (((1,), (0,)), ((), ())), preferred_element_type=F32)


def kernel(
    n, m, heads, factor,
    q_hbm, k_hbm, v_hbm, do_hbm, gains, lists,
    att_hbm, dq_hbm, dk_hbm, dv_hbm, gain_out,
    q_in, k_in, v_in, do_in, halo, back, ret, tail_acc,
    att_o, dq_o, dk_o, dv_o, p_s, ds_s, dor_s, gacc, g1, g2,
    in_sem, out_sem, hs_sem, hr_sem, bs_sem, br_sem, s1, r1, s2, r2,
):
    me = lax.axis_index("ctx")
    mf = lax.axis_index("fsdp")
    ins = ((q_hbm, q_in), (k_hbm, k_in), (v_hbm, v_in), (do_hbm, do_in))
    outs = ((att_o, att_hbm), (dq_o, dq_hbm), (dk_o, dk_hbm), (dv_o, dv_hbm))

    def cols(h):
        return pl.ds(pl.multiple_of(h * D, D), D)

    def in_copy(t, h):
        return pltpu.make_async_copy(ins[t][0].at[:, cols(h)], ins[t][1].at[h], in_sem.at[t, h])

    def out_copy(t, h):
        return pltpu.make_async_copy(outs[t][0].at[h], outs[t][1].at[:, cols(h)], out_sem.at[t, h])

    def halo_copy(h, kv, piece):
        src_row, dst_row, size = PIECES[piece]
        return pltpu.make_async_remote_copy(
            src_ref=(k_hbm, v_hbm)[kv].at[pl.ds(src_row, size), cols(h)],
            dst_ref=halo.at[h, kv, pl.ds(dst_row, size)],
            send_sem=hs_sem.at[h, kv, piece],
            recv_sem=hr_sem.at[h, kv, piece],
            device_id={"ctx": me + 1},
            device_id_type=MESH,
        )

    def back_copy(h):
        return pltpu.make_async_remote_copy(
            src_ref=back.at[h],
            dst_ref=ret.at[h],
            send_sem=bs_sem.at[h],
            recv_sem=br_sem.at[h],
            device_id={"ctx": me - 1},
            device_id_type=MESH,
        )

    def load_inputs(h, c):
        for t in (1, 0, 2, 3):
            in_copy(t, h).start()
        return c

    lax.fori_loop(0, heads, load_inputs, 0)

    barrier = pltpu.get_barrier_semaphore()

    def greet_ctx(k, c):
        pl.semaphore_signal(barrier, inc=1, device_id={"ctx": lax.rem(me + k, n)}, device_id_type=MESH)
        return c

    def greet_fsdp(k, c):
        pl.semaphore_signal(barrier, inc=1, device_id={"fsdp": lax.rem(mf + k, m)}, device_id_type=MESH)
        return c

    lax.fori_loop(1, n, greet_ctx, 0)
    lax.fori_loop(1, m, greet_fsdp, 0)
    pl.semaphore_wait(barrier, n - 1 + m - 1)

    @pl.when(me < n - 1)
    def _():
        def send(h, c):
            for piece in range(2):
                for kv in range(2):
                    halo_copy(h, kv, piece).start()
            return c

        lax.fori_loop(0, heads, send, 0)

    @pl.when(me == 0)
    def _():
        halo[...] = jnp.zeros_like(halo)

    @pl.when(me == n - 1)
    def _():
        ret[...] = jnp.zeros_like(ret)

    gacc[...] = jnp.zeros_like(gacc)
    inv_root = 1.0 / math.sqrt(D)
    c2 = math.log2(math.e) * inv_root
    gq = gains[0:1, :]
    gk = gains[1:2, :]
    go = gains[2:3, :]
    gq2 = gq * c2
    row_id = lax.broadcasted_iota(jnp.int32, (B, B), 0)
    col_id = lax.broadcasted_iota(jnp.int32, (B, B), 1)
    causal = row_id >= col_id

    def key_back(raw, dkn):
        scale = lax.rsqrt(rowmean(raw * raw) + EPS)
        unit = raw * scale
        inner = dkn * gk
        return scale * (inner - unit * rowmean(inner * unit)), unit

    def finish_tail(h):
        @pl.when(me < n - 1)
        def _():
            back_copy(h).wait_recv()

        for i, blk in enumerate(TAIL):
            rows = pl.ds(blk * B, B)
            raw = k_in[h, rows, :].astype(F32)
            dkn = tail_acc[h, 0, pl.ds(i * B, B), :] + ret[h, 0, pl.ds(i * B, B), :].astype(F32)
            grad, _ = key_back(raw, dkn)
            dk_o[h, rows, :] = grad.astype(BF16)
            dvv = tail_acc[h, 1, pl.ds(i * B, B), :] + ret[h, 1, pl.ds(i * B, B), :].astype(F32)
            dv_o[h, rows, :] = dvv.astype(BF16)
        out_copy(2, h).start()
        out_copy(3, h).start()

    def head(h, c):
        for t in range(4):
            in_copy(t, h).wait()
        kr = k_in[h].astype(F32)
        kb = (kr * lax.rsqrt(rowmean(kr * kr) + EPS) * gk).astype(BF16)
        qr = q_in[h].astype(F32)
        rq = lax.rsqrt(rowmean(qr * qr) + EPS)
        qs = (qr * rq * gq2).astype(BF16)
        qt = qs.T
        vb = v_in[h]

        @pl.when(me > 0)
        def _():
            for piece in range(2):
                for kv in range(2):
                    halo_copy(h, kv, piece).wait_recv()

        hr = halo[h, 0].astype(F32)
        hn = hr * lax.rsqrt(rowmean(hr * hr) + EPS)
        hb = (hn * gk).astype(BF16)
        hv = halo[h, 1]

        def kblk(u):
            return kb[u * B:(u + 1) * B] if u >= 0 else hb[HALO_AT[u] * B:(HALO_AT[u] + 1) * B]

        def vblk(u):
            return vb[u * B:(u + 1) * B] if u >= 0 else hv[HALO_AT[u] * B:(HALO_AT[u] + 1) * B]

        ones = jnp.ones((B, D), BF16)
        for b in range(6):
            rows = slice(b * B, (b + 1) * B)
            qb = qs[rows]
            keys = jnp.concatenate([kblk(u) for u, _ in WINDOW[b]], axis=0)
            vals = jnp.concatenate([vblk(u) for u, _ in WINDOW[b]], axis=0)
            s = dot_nt(qb, keys)
            ps = []
            for i, (u, slot) in enumerate(WINDOW[b]):
                e = jnp.exp2(s[:, i * B:(i + 1) * B])
                if slot == 0:
                    e = jnp.where(causal, e, 0.0)
                else:
                    e = e * jnp.where(lists[b, slot] >= 0, 1.0, 0.0).astype(F32)
                ps.append(e)
            pb = jnp.concatenate([e.astype(BF16) for e in ps], axis=1)
            vone = jnp.concatenate(
                [vals, jnp.concatenate([ones] * len(ps), axis=0)], axis=1)
            acc = dot_nn(pb, vone)
            r = 1.0 / acc[:, D:]
            out = acc[:, :D] * r
            att_o[h, pl.ds(b * B, B), :] = (out * go).astype(BF16)
            dout = do_in[h, pl.ds(b * B, B), :].astype(F32)
            gacc[2] += fold(dout * out)
            dor = (dout * go * r).astype(BF16)
            dor_s[pl.ds(b * B, B), :] = dor
            delta = jnp.sum(dor.astype(F32) * out, axis=-1, keepdims=True)
            dp = dot_nt(dor, vals)
            dss = []
            for i, (u, slot) in enumerate(WINDOW[b]):
                ds = (ps[i] * (dp[:, i * B:(i + 1) * B] - delta)).astype(BF16)
                dss.append(ds)
                at = pl.ds((BASE[u] + b - SEEN[u][0]) * B, B)
                p_s[at, :] = pb[:, i * B:(i + 1) * B]
                ds_s[at, :] = ds
            dqn = dot_nn(jnp.concatenate(dss, axis=1), keys) * inv_root
            raw = qr[rows]
            scale = rq[rows]
            unit = raw * scale
            gacc[0] += fold(dqn * unit)
            inner = dqn * gq
            grad = scale * (inner - unit * rowmean(inner * unit))
            dq_o[h, pl.ds(b * B, B), :] = grad.astype(BF16)
        out_copy(0, h).start()
        out_copy(1, h).start()

        dort = dor_s[...].T
        for u in KEYS:
            f, l = SEEN[u]
            qcols = slice(f * B, (l + 1) * B)
            at = pl.ds(BASE[u] * B, (l + 1 - f) * B)
            dku = (dot_nn(qt[:, qcols], ds_s[at, :]) * math.log(2.0)).T
            dvu = dot_nn(dort[:, qcols], p_s[at, :]).T
            if u < 0:
                i = HALO_AT[u]
                gacc[1] += fold(dku * hn[i * B:(i + 1) * B])
                back[h, 0, pl.ds(i * B, B), :] = dku.astype(BF16)
                back[h, 1, pl.ds(i * B, B), :] = dvu.astype(BF16)
                if u == -1:
                    @pl.when(me > 0)
                    def _():
                        back_copy(h).start()
            else:
                raw = k_in[h, pl.ds(u * B, B), :].astype(F32)
                if u in TAIL:
                    i = TAIL.index(u)
                    unit = raw * lax.rsqrt(rowmean(raw * raw) + EPS)
                    tail_acc[h, 0, pl.ds(i * B, B), :] = dku
                    tail_acc[h, 1, pl.ds(i * B, B), :] = dvu
                else:
                    grad, unit = key_back(raw, dku)
                    dk_o[h, pl.ds(u * B, B), :] = grad.astype(BF16)
                    dv_o[h, pl.ds(u * B, B), :] = dvu.astype(BF16)
                gacc[1] += fold(dku * unit)

        @pl.when(h >= 2)
        def _():
            finish_tail(h - 2)

        return c

    lax.fori_loop(0, heads, head, 0)

    g1[me] = jnp.concatenate(
        [jnp.sum(gacc[i], axis=0, keepdims=True) for i in range(3)] + [jnp.zeros((5, D), F32)], axis=0)

    def c1(k):
        return pltpu.make_async_remote_copy(
            src_ref=g1.at[me], dst_ref=g1.at[me], send_sem=s1.at[k], recv_sem=r1.at[me],
            device_id={"ctx": lax.rem(me + k, n)}, device_id_type=MESH)

    def w1(k):
        src = lax.rem(me + n - k, n)
        return pltpu.make_async_remote_copy(
            src_ref=g1.at[src], dst_ref=g1.at[src], send_sem=s1.at[k], recv_sem=r1.at[src],
            device_id={"ctx": src}, device_id_type=MESH)

    def c2_(k):
        return pltpu.make_async_remote_copy(
            src_ref=g2.at[mf], dst_ref=g2.at[mf], send_sem=s2.at[k], recv_sem=r2.at[mf],
            device_id={"fsdp": lax.rem(mf + k, m)}, device_id_type=MESH)

    def w2(k):
        src = lax.rem(mf + m - k, m)
        return pltpu.make_async_remote_copy(
            src_ref=g2.at[src], dst_ref=g2.at[src], send_sem=s2.at[k], recv_sem=r2.at[src],
            device_id={"fsdp": src}, device_id_type=MESH)

    def loop(count, fn):
        def body(k, c):
            fn(k)
            return c

        lax.fori_loop(1, count, body, 0)

    loop(n, lambda k: c1(k).start())
    if heads >= 2:
        finish_tail(heads - 2)
    loop(n, lambda k: w1(k).wait_recv())
    g2[mf] = lax.fori_loop(0, n, lambda i, a: a + g1[i], jnp.zeros((8, D), F32))
    loop(m, lambda k: c2_(k).start())
    finish_tail(heads - 1)
    loop(m, lambda k: w2(k).wait_recv())
    total = lax.fori_loop(0, m, lambda i, a: a + g2[i], jnp.zeros((8, D), F32))
    gain_out[...] = total[0:3] * factor

    loop(n, lambda k: c1(k).wait_send())
    loop(m, lambda k: c2_(k).wait_send())

    def drain(h, c):
        for t in range(4):
            out_copy(t, h).wait()

        @pl.when(me < n - 1)
        def _():
            for piece in range(2):
                for kv in range(2):
                    halo_copy(h, kv, piece).wait_send()

        @pl.when(me > 0)
        def _():
            back_copy(h).wait_send()

        return c

    lax.fori_loop(0, heads, drain, 0)


def local(n, m, queries, key_input, value_input, out_grad, norm_gains, block_lists):
    rows, width = queries.shape
    heads = width // D
    factor = 1.0 / math.sqrt(rows * n * heads * m)
    hbm = pl.BlockSpec(memory_space=pl.ANY)
    vmem = pl.BlockSpec(memory_space=pltpu.VMEM)
    smem = pl.BlockSpec(memory_space=pltpu.SMEM)
    big = jax.ShapeDtypeStruct((rows, width), BF16)
    hrows = pltpu.VMEM((heads, rows, D), BF16)
    hhalo = pltpu.VMEM((heads, 2, 3 * B, D), BF16)
    dma = pltpu.SemaphoreType.DMA
    return pl.pallas_call(
        functools.partial(kernel, n, m, heads, factor),
        out_shape=[big, big, big, big, jax.ShapeDtypeStruct((3, D), F32)],
        in_specs=[hbm, hbm, hbm, hbm, vmem, smem],
        out_specs=[hbm, hbm, hbm, hbm, vmem],
        scratch_shapes=[
            hrows, hrows, hrows, hrows,
            hhalo, hhalo, hhalo,
            pltpu.VMEM((heads, 2, 3 * B, D), F32),
            hrows, hrows, hrows, hrows,
            pltpu.VMEM((PAIRS * B, B), BF16),
            pltpu.VMEM((PAIRS * B, B), BF16),
            pltpu.VMEM((rows, D), BF16),
            pltpu.VMEM((3, 8, D), F32),
            pltpu.VMEM((n, 8, D), F32),
            pltpu.VMEM((m, 8, D), F32),
            dma((4, heads)), dma((4, heads)),
            dma((heads, 2, 2)), dma((heads, 2, 2)),
            dma((heads,)), dma((heads,)),
            dma((n,)), dma((n,)), dma((m,)), dma((m,)),
        ],
        compiler_params=pltpu.CompilerParams(
            collective_id=0, has_side_effects=True, vmem_limit_bytes=48 * 1024 * 1024),
        cost_estimate=pl.CostEstimate(
            flops=heads * PAIRS * 12 * B * B * D, bytes_accessed=rows * width * 16,
            transcendentals=heads * PAIRS * B * B),
        name="block_sparse_attention",
    )(queries, key_input, value_input, out_grad, norm_gains, block_lists)


def solution(mesh):
    n = mesh.shape["ctx"]
    m = mesh.shape["fsdp"]
    spec = P("ctx", "fsdp")
    return jax.shard_map(
        functools.partial(local, n, m),
        mesh=mesh,
        in_specs=(spec, spec, spec, spec, P(), P("ctx", None)),
        out_specs=(spec, spec, spec, spec, P()),
        check_vma=False,
    )
```

```python
import functools
import math

import jax
import jax.numpy as jnp
from jax import lax
from jax.experimental import pallas as pl
from jax.experimental.pallas import tpu as pltpu
from jax.sharding import PartitionSpec as P

EPS = 1e-06
B = 128
D = 128
F32 = jnp.float32
BF16 = jnp.bfloat16
MESH = pl.DeviceIdType.MESH

KEYS = (-2, -4, -1, 0, 1, 2, 3, 4, 5)
SEEN = {-2: (0, 0), -4: (0, 2), -1: (0, 5), 0: (0, 2), 1: (1, 3), 2: (2, 5), 3: (3, 5), 4: (4, 5), 5: (5, 5)}
BASE = {}
_total = 0
for _key in KEYS:
    BASE[_key] = _total
    _total += SEEN[_key][1] - SEEN[_key][0] + 1
PAIRS = _total
WINDOW = []
for _b in range(6):
    _g = _b - _b % 3
    _low = {0: -1, 3: 2}[_g]
    _far = {0: -4, 3: -1}[_g]
    if _b % 3 == 0:
        WINDOW.append(((_b - 2, 2), (_far, 4), (_low, 1), (_b, 0)))
    elif _b % 3 == 1:
        WINDOW.append(((_far, 4), (_low, 2), (_b - 1, 1), (_b, 0)))
    else:
        WINDOW.append(((_far, 4), (_low, 3), (_b - 2, 2), (_b - 1, 1), (_b, 0)))
ORDER = ((-2, -4, -1, 0, 1, 2), (1, -1, 2, 3, 4, 5))
HALO_AT = {-4: 0, -2: 1, -1: 2}
TAIL = (2, 4, 5)
PIECES = ((2 * B, 0, B), (4 * B, B, 2 * B))


def rowmean(x):
    return jnp.sum(x, axis=-1, keepdims=True) * (1.0 / D)


def fold(x):
    return jnp.sum(x.reshape(x.shape[0] // 8, 8, D), axis=0)


def dot_nt(a, b):
    return lax.dot_general(a, b, (((1,), (1,)), ((), ())), preferred_element_type=F32)


def dot_nn(a, b):
    return lax.dot_general(a, b, (((1,), (0,)), ((), ())), preferred_element_type=F32)


def kernel(
    n, m, heads, factor,
    q_hbm, k_hbm, v_hbm, do_hbm, gains, lists,
    att_hbm, dq_hbm, dk_hbm, dv_hbm, gain_out,
    q_in, k_in, v_in, do_in, halo, back, ret, tail_acc,
    att_o, dq_o, dk_o, dv_o, p_s, ds_s, dor_s, gacc, g1, g2,
    nk_s, nq_s, rq_s, delta_s, hn_s, qs_s, qt_s, dort_s, kw, vw, ktw, vtw, pb_s, dsb_s,
    in_sem, out_sem, hs_sem, hr_sem, bs_sem, br_sem, s1, r1, s2, r2,
):
    me = lax.axis_index("ctx")
    mf = lax.axis_index("fsdp")
    ins = ((q_hbm, q_in), (k_hbm, k_in), (v_hbm, v_in), (do_hbm, do_in))
    outs = ((att_o, att_hbm), (dq_o, dq_hbm), (dk_o, dk_hbm), (dv_o, dv_hbm))

    def cols(h):
        return pl.ds(pl.multiple_of(h * D, D), D)

    def in_copy(t, h):
        return pltpu.make_async_copy(ins[t][0].at[:, cols(h)], ins[t][1].at[h], in_sem.at[t, h])

    def out_copy(t, h):
        return pltpu.make_async_copy(outs[t][0].at[h], outs[t][1].at[:, cols(h)], out_sem.at[t, h])

    def halo_copy(h, kv, piece):
        src_row, dst_row, size = PIECES[piece]
        return pltpu.make_async_remote_copy(
            src_ref=(k_hbm, v_hbm)[kv].at[pl.ds(src_row, size), cols(h)],
            dst_ref=halo.at[h, kv, pl.ds(dst_row, size)],
            send_sem=hs_sem.at[h, kv, piece],
            recv_sem=hr_sem.at[h, kv, piece],
            device_id={"ctx": me + 1},
            device_id_type=MESH,
        )

    def back_copy(h):
        return pltpu.make_async_remote_copy(
            src_ref=back.at[h],
            dst_ref=ret.at[h],
            send_sem=bs_sem.at[h],
            recv_sem=br_sem.at[h],
            device_id={"ctx": me - 1},
            device_id_type=MESH,
        )

    def load_inputs(h, c):
        for t in (1, 0, 2, 3):
            in_copy(t, h).start()
        return c

    lax.fori_loop(0, heads, load_inputs, 0)

    barrier = pltpu.get_barrier_semaphore()

    def greet_ctx(k, c):
        pl.semaphore_signal(barrier, inc=1, device_id={"ctx": lax.rem(me + k, n)}, device_id_type=MESH)
        return c

    def greet_fsdp(k, c):
        pl.semaphore_signal(barrier, inc=1, device_id={"fsdp": lax.rem(mf + k, m)}, device_id_type=MESH)
        return c

    lax.fori_loop(1, n, greet_ctx, 0)
    lax.fori_loop(1, m, greet_fsdp, 0)
    pl.semaphore_wait(barrier, n - 1 + m - 1)

    @pl.when(me < n - 1)
    def _():
        def send(h, c):
            for piece in range(2):
                for kv in range(2):
                    halo_copy(h, kv, piece).start()
            return c

        lax.fori_loop(0, heads, send, 0)

    @pl.when(me == 0)
    def _():
        halo[...] = jnp.zeros_like(halo)

    @pl.when(me == n - 1)
    def _():
        ret[...] = jnp.zeros_like(ret)

    gacc[...] = jnp.zeros_like(gacc)
    vw[:, :, D:] = jnp.ones((2, 6 * B, D), BF16)
    inv_root = 1.0 / math.sqrt(D)
    c2 = math.log2(math.e) * inv_root
    gq = gains[0:1, :]
    gk = gains[1:2, :]
    go = gains[2:3, :]
    gq2 = gq * c2
    row_id = lax.broadcasted_iota(jnp.int32, (B, B), 0)
    col_id = lax.broadcasted_iota(jnp.int32, (B, B), 1)
    causal = row_id >= col_id

    def key_back(raw, dkn):
        scale = lax.rsqrt(rowmean(raw * raw) + EPS)
        unit = raw * scale
        inner = dkn * gk
        return scale * (inner - unit * rowmean(inner * unit)), unit

    def finish_tail(h):
        @pl.when(me < n - 1)
        def _():
            back_copy(h).wait_recv()

        for i, blk in enumerate(TAIL):
            rows = pl.ds(blk * B, B)
            raw = k_in[h, rows, :].astype(F32)
            dkn = tail_acc[h, 0, pl.ds(i * B, B), :] + ret[h, 0, pl.ds(i * B, B), :].astype(F32)
            grad, _ = key_back(raw, dkn)
            dk_o[h, rows, :] = grad.astype(BF16)
            dvv = tail_acc[h, 1, pl.ds(i * B, B), :] + ret[h, 1, pl.ds(i * B, B), :].astype(F32)
            dv_o[h, rows, :] = dvv.astype(BF16)
        out_copy(2, h).start()
        out_copy(3, h).start()

    def head(h, c):
        for t in range(4):
            in_copy(t, h).wait()
        kr = k_in[h].astype(F32)
        nk_s[...] = kr * lax.rsqrt(rowmean(kr * kr) + EPS)
        qr = q_in[h].astype(F32)
        rq = lax.rsqrt(rowmean(qr * qr) + EPS)
        nq = qr * rq
        nq_s[...] = nq
        rq_s[...] = jnp.broadcast_to(rq, nq.shape)
        qs = (nq * gq2).astype(BF16)
        qs_s[...] = qs
        qt_s[...] = qs.T

        @pl.when(me > 0)
        def _():
            for piece in range(2):
                for kv in range(2):
                    halo_copy(h, kv, piece).wait_recv()

        hr = halo[h, 0].astype(F32)
        hn_s[...] = hr * lax.rsqrt(rowmean(hr * hr) + EPS)
        for u in KEYS:
            if u >= 0:
                kb = (nk_s[pl.ds(u * B, B), :] * gk).astype(BF16)
                vb = v_in[h, pl.ds(u * B, B), :]
            else:
                kb = (hn_s[pl.ds(HALO_AT[u] * B, B), :] * gk).astype(BF16)
                vb = halo[h, 1, pl.ds(HALO_AT[u] * B, B), :]
            kt = kb.T
            vt = vb.T
            for g in range(2):
                if u in ORDER[g]:
                    at = pl.ds(ORDER[g].index(u) * B, B)
                    kw[g, at, :] = kb
                    vw[g, at, 0:D] = vb
                    ktw[g, :, at] = kt
                    vtw[g, :, at] = vt

        def window(b):
            order = ORDER[b // 3]
            return b // 3, order.index(WINDOW[b][0][0]) * B, len(WINDOW[b]) * B

        for b in range(6):
            g, start, size = window(b)
            s = dot_nn(qs_s[pl.ds(b * B, B), :], ktw[g, :, pl.ds(start, size)])
            for i, (u, slot) in enumerate(WINDOW[b]):
                e = jnp.exp2(s[:, i * B:(i + 1) * B])
                if slot == 0:
                    e = jnp.where(causal, e, 0.0)
                else:
                    e = e * jnp.where(lists[b, slot] >= 0, 1.0, 0.0).astype(F32)
                low = e.astype(BF16)
                pb_s[b, :, pl.ds(i * B, B)] = low
                p_s[pl.ds((BASE[u] + b - SEEN[u][0]) * B, B), :] = low

        dout_sum = jnp.zeros((8, D), F32)
        for b in range(6):
            g, start, size = window(b)
            acc = dot_nn(pb_s[b, :, pl.ds(0, size)], vw[g, pl.ds(start, size), :])
            r = 1.0 / acc[:, D:]
            out = acc[:, :D] * r
            att_o[h, pl.ds(b * B, B), :] = (out * go).astype(BF16)
            dout = do_in[h, pl.ds(b * B, B), :].astype(F32)
            dout_sum += fold(dout * out)
            dor = (dout * go * r).astype(BF16)
            dor_s[pl.ds(b * B, B), :] = dor
            dort_s[:, pl.ds(b * B, B)] = dor.T
            delta = jnp.sum(dor.astype(F32) * out, axis=-1, keepdims=True)
            delta_s[pl.ds(b * B, B), :] = jnp.broadcast_to(delta, out.shape)
        gacc[2] += dout_sum
        out_copy(0, h).start()

        for b in range(6):
            g, start, size = window(b)
            dp = dot_nn(dor_s[pl.ds(b * B, B), :], vtw[g, :, pl.ds(start, size)])
            delta = delta_s[pl.ds(b * B, B), :]
            for i, (u, slot) in enumerate(WINDOW[b]):
                p = pb_s[b, :, pl.ds(i * B, B)].astype(F32)
                ds = (p * (dp[:, i * B:(i + 1) * B] - delta)).astype(BF16)
                dsb_s[b, :, pl.ds(i * B, B)] = ds
                ds_s[pl.ds((BASE[u] + b - SEEN[u][0]) * B, B), :] = ds

        key_sum = jnp.zeros((8, D), F32)
        for u in KEYS:
            f, l = SEEN[u]
            qcols = pl.ds(f * B, (l + 1 - f) * B)
            at = pl.ds(BASE[u] * B, (l + 1 - f) * B)
            dku = (dot_nn(qt_s[:, qcols], ds_s[at, :]) * math.log(2.0)).T
            dvu = dot_nn(dort_s[:, qcols], p_s[at, :]).astype(BF16).T
            if u < 0:
                i = HALO_AT[u]
                key_sum += fold(dku * hn_s[pl.ds(i * B, B), :])
                back[h, 0, pl.ds(i * B, B), :] = dku.astype(BF16)
                back[h, 1, pl.ds(i * B, B), :] = dvu
                if u == -1:
                    @pl.when(me > 0)
                    def _():
                        back_copy(h).start()
            else:
                key_sum += fold(dku * nk_s[pl.ds(u * B, B), :])
                if u in TAIL:
                    i = TAIL.index(u)
                    tail_acc[h, 0, pl.ds(i * B, B), :] = dku
                    tail_acc[h, 1, pl.ds(i * B, B), :] = dvu.astype(F32)
                else:
                    grad, unit = key_back(k_in[h, pl.ds(u * B, B), :].astype(F32), dku)
                    dk_o[h, pl.ds(u * B, B), :] = grad.astype(BF16)
                    dv_o[h, pl.ds(u * B, B), :] = dvu
        gacc[1] += key_sum

        query_sum = jnp.zeros((8, D), F32)
        for b in range(6):
            g, start, size = window(b)
            rows = pl.ds(b * B, B)
            dqn = dot_nn(dsb_s[b, :, pl.ds(0, size)], kw[g, pl.ds(start, size), :]) * inv_root
            unit = nq_s[rows, :]
            query_sum += fold(dqn * unit)
            inner = dqn * gq
            grad = rq_s[rows, :] * (inner - unit * rowmean(inner * unit))
            dq_o[h, rows, :] = grad.astype(BF16)
        gacc[0] += query_sum
        out_copy(1, h).start()

        @pl.when(h >= 2)
        def _():
            finish_tail(h - 2)

        return c

    lax.fori_loop(0, heads, head, 0)

    g1[me] = jnp.concatenate(
        [jnp.sum(gacc[i], axis=0, keepdims=True) for i in range(3)] + [jnp.zeros((5, D), F32)], axis=0)

    def c1(k):
        return pltpu.make_async_remote_copy(
            src_ref=g1.at[me], dst_ref=g1.at[me], send_sem=s1.at[k], recv_sem=r1.at[me],
            device_id={"ctx": lax.rem(me + k, n)}, device_id_type=MESH)

    def w1(k):
        src = lax.rem(me + n - k, n)
        return pltpu.make_async_remote_copy(
            src_ref=g1.at[src], dst_ref=g1.at[src], send_sem=s1.at[k], recv_sem=r1.at[src],
            device_id={"ctx": src}, device_id_type=MESH)

    def c2_(k):
        return pltpu.make_async_remote_copy(
            src_ref=g2.at[mf], dst_ref=g2.at[mf], send_sem=s2.at[k], recv_sem=r2.at[mf],
            device_id={"fsdp": lax.rem(mf + k, m)}, device_id_type=MESH)

    def w2(k):
        src = lax.rem(mf + m - k, m)
        return pltpu.make_async_remote_copy(
            src_ref=g2.at[src], dst_ref=g2.at[src], send_sem=s2.at[k], recv_sem=r2.at[src],
            device_id={"fsdp": src}, device_id_type=MESH)

    def loop(count, fn):
        def body(k, c):
            fn(k)
            return c

        lax.fori_loop(1, count, body, 0)

    loop(n, lambda k: c1(k).start())
    if heads >= 2:
        finish_tail(heads - 2)
    loop(n, lambda k: w1(k).wait_recv())
    g2[mf] = lax.fori_loop(0, n, lambda i, a: a + g1[i], jnp.zeros((8, D), F32))
    loop(m, lambda k: c2_(k).start())
    finish_tail(heads - 1)
    loop(m, lambda k: w2(k).wait_recv())
    total = lax.fori_loop(0, m, lambda i, a: a + g2[i], jnp.zeros((8, D), F32))
    gain_out[...] = total[0:3] * factor

    loop(n, lambda k: c1(k).wait_send())
    loop(m, lambda k: c2_(k).wait_send())

    def drain(h, c):
        for t in range(4):
            out_copy(t, h).wait()

        @pl.when(me < n - 1)
        def _():
            for piece in range(2):
                for kv in range(2):
                    halo_copy(h, kv, piece).wait_send()

        @pl.when(me > 0)
        def _():
            back_copy(h).wait_send()

        return c

    lax.fori_loop(0, heads, drain, 0)


def local(n, m, queries, key_input, value_input, out_grad, norm_gains, block_lists):
    rows, width = queries.shape
    heads = width // D
    factor = 1.0 / math.sqrt(rows * n * heads * m)
    hbm = pl.BlockSpec(memory_space=pl.ANY)
    vmem = pl.BlockSpec(memory_space=pltpu.VMEM)
    smem = pl.BlockSpec(memory_space=pltpu.SMEM)
    big = jax.ShapeDtypeStruct((rows, width), BF16)
    hrows = pltpu.VMEM((heads, rows, D), BF16)
    hhalo = pltpu.VMEM((heads, 2, 3 * B, D), BF16)
    frows = pltpu.VMEM((rows, D), F32)
    dma = pltpu.SemaphoreType.DMA
    return pl.pallas_call(
        functools.partial(kernel, n, m, heads, factor),
        out_shape=[big, big, big, big, jax.ShapeDtypeStruct((3, D), F32)],
        in_specs=[hbm, hbm, hbm, hbm, vmem, smem],
        out_specs=[hbm, hbm, hbm, hbm, vmem],
        scratch_shapes=[
            hrows, hrows, hrows, hrows,
            hhalo, hhalo, hhalo,
            pltpu.VMEM((heads, 2, 3 * B, D), F32),
            hrows, hrows, hrows, hrows,
            pltpu.VMEM((PAIRS * B, B), BF16),
            pltpu.VMEM((PAIRS * B, B), BF16),
            pltpu.VMEM((rows, D), BF16),
            pltpu.VMEM((3, 8, D), F32),
            pltpu.VMEM((n, 8, D), F32),
            pltpu.VMEM((m, 8, D), F32),
            frows, frows, frows, frows,
            pltpu.VMEM((3 * B, D), F32),
            pltpu.VMEM((rows, D), BF16),
            pltpu.VMEM((D, rows), BF16),
            pltpu.VMEM((D, rows), BF16),
            pltpu.VMEM((2, 6 * B, D), BF16),
            pltpu.VMEM((2, 6 * B, 2 * D), BF16),
            pltpu.VMEM((2, D, 6 * B), BF16),
            pltpu.VMEM((2, D, 6 * B), BF16),
            pltpu.VMEM((6, B, 5 * B), BF16),
            pltpu.VMEM((6, B, 5 * B), BF16),
            dma((4, heads)), dma((4, heads)),
            dma((heads, 2, 2)), dma((heads, 2, 2)),
            dma((heads,)), dma((heads,)),
            dma((n,)), dma((n,)), dma((m,)), dma((m,)),
        ],
        compiler_params=pltpu.CompilerParams(
            collective_id=0, has_side_effects=True, vmem_limit_bytes=60 * 1024 * 1024),
        cost_estimate=pl.CostEstimate(
            flops=heads * PAIRS * 12 * B * B * D, bytes_accessed=rows * width * 16,
            transcendentals=heads * PAIRS * B * B),
        name="block_sparse_attention",
    )(queries, key_input, value_input, out_grad, norm_gains, block_lists)


def solution(mesh):
    n = mesh.shape["ctx"]
    m = mesh.shape["fsdp"]
    spec = P("ctx", "fsdp")
    return jax.shard_map(
        functools.partial(local, n, m),
        mesh=mesh,
        in_specs=(spec, spec, spec, spec, P(), P("ctx", None)),
        out_specs=(spec, spec, spec, spec, P()),
        check_vma=False,
    )
```
